256 devices in a mesh: dp: 32 (over y, z), mp: 8 (over x, core).
Axes of the slice: x: 4, y: 4, z: 8, core: 2. Of those that a mesh axis runs over, the one named last changes fastest.
Arguments:
- tokens: bfloat16 [4096, 4096], P('dp', 'mp'), may hold values from -6 to 6
- cotangent: bfloat16 [4096, 4096], P('dp', 'mp'), may hold values from -6 to 6
- language: int32 [4096, 1], P('dp'), may hold values from 0 to 7; in each aligned block of 128 rows (0 to 127, 128 to 255, ...) at most 24 rows name the same one
- owner: int32 [8], replicated, may hold values from 0 to 7, each once
- w_in: bfloat16 [4096, 65536], P(None, ('dp', 'mp')), may hold values from -0.09375 to 0.09375
- w_out: bfloat16 [65536, 4096], P(('dp', 'mp')), may hold values from -0.0625 to 0.0625
Outputs:
- ffn_out: bfloat16 [4096, 4096], P('dp', 'mp')
- grad_tokens: bfloat16 [4096, 4096], P('dp', 'mp')
- grad_in: bfloat16 [4096, 65536], P(None, ('dp', 'mp'))
- grad_out: bfloat16 [65536, 4096], P(('dp', 'mp'))
The draws below stay inside these ranges and needn't reach their ends.
Inputs may be any that keep to these rules, and one draw needn't show every extreme that they name: In each aligned block of 128 rows (the rows of one index of dp) no language appears more than 24 times; some language appears exactly 24 times in some block; every language appears somewhere. `owner`: each slot 0 to 7 belongs to exactly one language.
All inputs are finite; a program needn't handle non-finite values.
Results may differ from the reference program's by a relative error of at most 0.019.
Values may be sent and summed in bfloat16 or wider, within the bound.
A program may use at most 128 MiB of HBM per device.

```python
import math
import jax
import jax.numpy as jnp
import numpy as np
from jax import lax

D = 4096
FF = 8192
GROUP = 4
TOK_DEV = 128
LANGS = 8
CAP = 24
TOKENS = 4096
N_DP = 32
N_MP = 8


def steps_of(rng, extent, shards, least, high):
    loudness = 1.0
    for dim, shards_of in shards:
        heights = jax.random.uniform(jax.random.fold_in(jax.random.fold_in(rng, 6), dim), (shards_of,), jnp.float32, least / len(shards), high / len(shards))
        loudness = loudness * jnp.repeat(jnp.exp(heights), extent[dim] // shards_of).reshape((-1,) + (1,) * (len(extent) - 1 - dim))
    return loudness


def assign_block(own_key, own, number, rows, number_of, top, reach, slope):
    ranking = jax.random.permutation(own_key, number_of)
    crowded, ordinary = load_shares(number_of, rows * top, reach, slope, True), load_shares(number_of, rows * top, reach, slope, False)
    places = jnp.arange(number_of)

    def named(sizes, turn):
        used = int((sizes > 0).sum())
        fixed = max(1, used // 4)
        passed = fixed + (places - fixed + turn * (used - fixed)) % max(1, number_of - fixed)
        return jnp.zeros((number_of,), jnp.int32).at[ranking[jnp.where(places < fixed, places, passed)]].set(jnp.asarray(sizes, jnp.int32))

    sizes = jnp.where(number % 4 == 0, named(crowded, number // 4), named(ordinary, number - number // 4 - 1))
    mixed = jax.random.permutation(jax.random.fold_in(own, 3), number_of)
    source_of, receiver = mixed[0:number_of // 2 * 2:2], mixed[1:number_of // 2 * 2:2]
    slack = jnp.minimum(sizes[source_of] - 1, reach - sizes[receiver]) // 2
    slack = jnp.where((source_of == ranking[0]) | (receiver == ranking[0]) | (sizes[receiver] == 0), 0, jnp.maximum(slack, 0))
    passed = jax.random.randint(jax.random.fold_in(own, 4), (number_of // 2,), 0, 1 << 20) % (slack + 1)
    sizes = sizes.at[source_of].add(-passed).at[receiver].add(passed)
    labels = jnp.searchsorted(jnp.cumsum(sizes), jnp.arange(rows * top), side="right").astype(jnp.int32)
    grid = labels.reshape(top, rows).T
    grid = grid[jax.random.permutation(jax.random.fold_in(own, 1), rows)]
    turn = jax.random.randint(jax.random.fold_in(own, 2), (rows, 1), 0, top)
    return jnp.take_along_axis(grid, (jnp.arange(top)[None, :] + turn) % top, axis=1)


def load_shares(amount, total, most, skew, full):
    portions = [(1 << 20) // math.isqrt(rank ** skew) + 1 for rank in range(1, amount + 1)]
    largest = most if full else min(most, max(-(-total // amount), total * portions[0] // sum(portions)))
    least = 1 if total - largest >= amount - 1 else 0
    counts, spare = [largest] + [least] * (amount - 1), total - largest - least * (amount - 1)
    while spare > 0:
        candidates = [i for i in range(1, amount) if counts[i] < largest] or [i for i in range(1, amount) if counts[i] < most]
        whole, left = sum([portions[i] for i in candidates]), spare
        for i in candidates:
            more = min(most - counts[i], max(1, left * portions[i] // whole), spare)
            counts[i] = counts[i] + more
            spare = spare - more
    return np.array(counts)


def normal_values(own_key, dims, width, limit, shards=(), held_as=jnp.bfloat16):
    gain = steps_of(own_key, dims, shards, -0.22, 0.18) if shards else 1.0
    values = jax.random.normal(own_key, dims, jnp.float32) * width * gain
    return jnp.minimum(jnp.maximum(values, -limit), limit).astype(held_as)


def setup_inputs(seed: int = 0) -> dict:
    key_list = jax.random.split(jax.random.key(seed), 7)
    tokens = normal_values(key_list[0], (TOKENS, D), 1.0, 6.0, ((0, 32), (1, 8)))
    cotangent = normal_values(key_list[1], (TOKENS, D), 1.0, 6.0, ((0, 32), (1, 8)))
    language_keys = jax.random.split(jax.random.fold_in(key_list[2], 1), TOKENS // TOK_DEV)
    language_turns = jax.random.permutation(jax.random.fold_in(key_list[2], 3), TOKENS // TOK_DEV)
    language = jax.vmap(lambda own, number: assign_block(jax.random.fold_in(key_list[2], 2), own, number, TOK_DEV, LANGS, 1, CAP, 2))(language_keys, language_turns).reshape((TOKENS, 1))
    owner = jax.random.permutation(key_list[3], LANGS).astype(jnp.int32)
    w_in = normal_values(key_list[4], (D, LANGS * FF), D ** -0.5, 0.09375, ((1, 256),))
    w_out = normal_values(key_list[5], (LANGS * FF, D), FF ** -0.5, 0.0625, ((0, 256),))
    return dict(tokens=tokens, cotangent=cotangent, language=language, owner=owner, w_in=w_in, w_out=w_out)


ROOT_HALF = 0.7071067811865476
INV_ROOT_TAU = 0.3989422804014327


def gelu_pair(hidden):
    normal_cdf = 0.5 * (1.0 + lax.erf(hidden * ROOT_HALF))
    return hidden * normal_cdf, normal_cdf + hidden * jnp.exp(-0.5 * hidden * hidden) * INV_ROOT_TAU


def reference(tokens, cotangent, language, owner, w_in, w_out):
    blocks = GROUP * N_MP
    block_width = FF // blocks
    slot_rows = N_DP * CAP
    row_lang = language[:, 0]
    lang_hit = (row_lang[:, None] == jnp.arange(LANGS, dtype=jnp.int32)[None, :]).astype(jnp.int32)
    row_rank = jnp.sum((jnp.cumsum(lang_hit, axis=0) - 1) * lang_hit, axis=1).astype(jnp.int32)
    row_table = jnp.full((LANGS, slot_rows), TOKENS, jnp.int32).at[row_lang, row_rank].set(jnp.arange(TOKENS, dtype=jnp.int32))
    tok_pad = jnp.concatenate([tokens, jnp.zeros((1, D), tokens.dtype)], axis=0)
    cot_pad = jnp.concatenate([cotangent, jnp.zeros((1, D), cotangent.dtype)], axis=0)

    def language_pass(lang_index):
        row_ids = row_table[lang_index]
        src_rows = tok_pad[row_ids]
        cot_rows = cot_pad[row_ids]
        col_start = (owner[lang_index] * FF).astype(jnp.int32)
        w_first = lax.dynamic_slice_in_dim(w_in, col_start, FF, 1)
        w_second = lax.dynamic_slice_in_dim(w_out, col_start, FF, 0)
        hidden = jnp.dot(src_rows, w_first, preferred_element_type=jnp.float32)
        act_value, act_slope = gelu_pair(hidden)
        act = act_value.astype(jnp.bfloat16)
        act_grad = lax.dot_general(cot_rows, w_second, (((1,), (1,)), ((), ())), preferred_element_type=jnp.float32)
        hidden_grad = (act_grad * act_slope).astype(jnp.bfloat16)
        grad_first = lax.dot_general(src_rows, hidden_grad, (((0,), (0,)), ((), ())), preferred_element_type=jnp.float32).astype(jnp.bfloat16)
        grad_second = lax.dot_general(act, cot_rows, (((0,), (0,)), ((), ())), preferred_element_type=jnp.float32).astype(jnp.bfloat16)
        act_blocks = act.reshape(slot_rows, blocks, block_width).transpose(1, 0, 2)
        grad_blocks = hidden_grad.reshape(slot_rows, blocks, block_width).transpose(1, 0, 2)
        first_blocks = w_first.reshape(D, blocks, block_width).transpose(1, 0, 2)
        second_blocks = w_second.reshape(blocks, block_width, D)

        def add_block(running, block_data):
            act_block, grad_block, first_block, second_block = block_data
            out_block = jnp.dot(act_block, second_block, preferred_element_type=jnp.float32).astype(jnp.bfloat16)
            back_block = lax.dot_general(grad_block, first_block, (((1,), (1,)), ((), ())), preferred_element_type=jnp.float32).astype(jnp.bfloat16)
            out_block, back_block = lax.optimization_barrier((out_block, back_block))
            return (running[0] + out_block.astype(jnp.float32), running[1] + back_block.astype(jnp.float32)), None

        zero_sum = jnp.zeros((slot_rows, D), jnp.float32)
        (out_sum, back_sum), _ = lax.scan(add_block, (zero_sum, zero_sum), (act_blocks, grad_blocks, first_blocks, second_blocks))
        return out_sum, back_sum, grad_first, grad_second

    out_all, back_all, first_all, second_all = lax.map(language_pass, jnp.arange(LANGS, dtype=jnp.int32))
    flat_table = row_table.reshape(-1)
    ffn_out = jnp.zeros((TOKENS + 1, D), jnp.float32).at[flat_table].set(out_all.reshape(-1, D))[:TOKENS].astype(jnp.bfloat16)
    grad_tokens = jnp.zeros((TOKENS + 1, D), jnp.float32).at[flat_table].set(back_all.reshape(-1, D))[:TOKENS].astype(jnp.bfloat16)
    grad_in = jnp.zeros((LANGS, D, FF), jnp.bfloat16).at[owner].set(first_all).transpose(1, 0, 2).reshape(D, LANGS * FF)
    grad_out = jnp.zeros((LANGS, FF, D), jnp.bfloat16).at[owner].set(second_all).reshape(LANGS * FF, D)
    return ffn_out, grad_tokens, grad_in, grad_out
```

```python
import jax
import jax.numpy as jnp
from jax import lax
from jax.experimental import pallas as pl
from jax.experimental.pallas import tpu as pltpu
from jax.sharding import PartitionSpec as P

MESH = pl.DeviceIdType.MESH
ROOT_HALF = 0.7071067811865476
INV_ROOT_TAU = 0.3989422804014327

NY, NZ, NX, NC = 4, 8, 4, 2
NP = NX * NC
BF = jnp.bfloat16
F32 = jnp.float32


def gelu_pair(hidden):
    normal_cdf = 0.5 * (1.0 + lax.erf(hidden * ROOT_HALF))
    return (
        hidden * normal_cdf,
        normal_cdf + hidden * jnp.exp(-0.5 * hidden * hidden) * INV_ROOT_TAU,
    )


def z_step(i):
    return ((i + 1) // 2) * (2 * (i % 2) - 1)


def nt_dot(a, b):
    return lax.dot_general(a, b, (((1,), (1,)), ((), ())), preferred_element_type=F32)


def kernel(
    tok, cot, lang, owner, w_in, w_out,
    ffn, gtok, grad_in, grad_out,
    w1, w2, pack, yrecv, zsend, gath, act, hgrad, part, srecv, acc, xrecv, zrecv, ysend, yback,
    gi, go,
    w_sem, g_sem, y_sem, z_sem, x_sem, s_sem, ps_sem, px_sem, pz_sem, py_sem,
):
    dp, mp = lax.axis_index("dp"), lax.axis_index("mp")
    y, z = dp // NZ, dp % NZ
    x, c = mp // NC, mp % NC
    rows, feat = tok.shape
    cell_rows = pack.shape[1]
    cap = cell_rows // 2
    chunk = NY * cap
    half = chunk // 2
    xr, xl, xo = (x + 1) % NX, (x + NX - 1) % NX, (x + 2) % NX
    sib = {"dp": dp, "mp": x * NC + 1 - c}
    right = {"dp": dp, "mp": xr * NC + c}
    left = {"dp": dp, "mp": xl * NC + c}

    def at_y(k):
        return {"dp": ((y + k) % NY) * NZ + z, "mp": mp}

    def at_z(k):
        return {"dp": y * NZ + (z + k + NZ) % NZ, "mp": mp}

    def remote(src, dst, sems, where, device):
        return pltpu.make_async_remote_copy(
            src_ref=src,
            dst_ref=dst,
            send_sem=sems.at[(0, *where)],
            recv_sem=sems.at[(1, *where)],
            device_id=device,
            device_id_type=MESH,
        )

    load1 = pltpu.make_async_copy(w_in, w1, w_sem.at[0])
    load2 = pltpu.make_async_copy(w_out, w2, w_sem.at[1])
    load1.start()
    load2.start()

    barrier = pltpu.get_barrier_semaphore()
    partners = [sib, right, left]
    partners += [at_y(k) for k in range(1, NY)] + [at_z(k) for k in range(1, NZ)]
    for device in partners:
        pl.semaphore_signal(barrier, inc=1, device_id=device, device_id_type=MESH)

    langs = owner.shape[1]
    hit = lang[...] == lax.broadcasted_iota(jnp.int32, (rows, langs), 1)
    lower = (
        lax.broadcasted_iota(jnp.int32, (rows, rows), 1)
        < lax.broadcasted_iota(jnp.int32, (rows, rows), 0)
    )
    before = jnp.dot(
        jnp.where(lower, 1.0, 0.0).astype(BF),
        jnp.where(hit, 1.0, 0.0).astype(BF),
        preferred_element_type=F32,
    )
    cell = jnp.sum(
        jnp.where(hit, before + owner[...].astype(F32) * cap, 0.0), axis=1, keepdims=True
    )
    cells = langs * cap
    place = jnp.where(
        cell.astype(jnp.int32) == lax.broadcasted_iota(jnp.int32, (rows, cells), 1), 1.0, 0.0
    )
    place_t = jnp.transpose(place).astype(BF)
    place = place.astype(BF)
    packed_x = jnp.dot(place_t, tok[...], preferred_element_type=F32).astype(BF)
    packed_g = jnp.dot(place_t, cot[...], preferred_element_type=F32).astype(BF)
    pack[:, :, :feat] = packed_x.reshape(NY, cell_rows, feat)
    pack[:, :, feat:] = packed_g.reshape(NY, cell_rows, feat)

    pl.semaphore_wait(barrier, len(partners))

    def y_copy(k):
        return remote(pack.at[(y + k) % NY], yrecv.at[k], y_sem, (k,), at_y(k))

    for k in range(1, NY):
        y_copy(k).start()
    yrecv[0] = pack[y]
    for k in range(1, NY):
        y_copy(k).wait_recv()
    for h in range(2):
        for col in (0, feat):
            block = jnp.concatenate(
                [
                    yrecv[k, :, col : col + feat].astype(F32)[h * cap : (h + 1) * cap]
                    for k in range(NY)
                ],
                axis=0,
            ).astype(BF)
            zsend[h, :, :, col : col + feat] = block.reshape(2, half, feat)

    half_z = NZ // 2

    def z_copy(i):
        to = (z - z_step(i) + NZ) % NZ
        return remote(
            zsend.at[to // half_z], gath.at[i, mp], z_sem, (i,), {"dp": y * NZ + to, "mp": mp}
        )

    @pl.loop(1, NZ)
    def _(i):
        z_copy(i).start()

    gath[0, mp] = zsend[z // half_z]

    def g_copy(kind, i):
        if kind == 0:
            return remote(gath.at[i, mp], gath.at[i, mp], x_sem, (0, i), right)
        if kind == 1:
            return remote(gath.at[i, mp], gath.at[i, mp], x_sem, (1, i), left)
        if kind == 2:
            src = gath.at[i, xl * NC + c, 0]
            return remote(src, src, x_sem, (2, i), right)
        src = gath.at[i, xr * NC + c, 1]
        return remote(src, src, x_sem, (3, i), left)

    def s_copy(kind, i):
        src = gath.at[i, (x, xl, xr, xo)[kind] * NC + c]
        return remote(src, src, s_sem, (kind, i), sib)

    def ps_copy(i):
        return remote(part.at[i], srecv.at[i], ps_sem, (i,), sib)

    def p_copy(kind, i):
        where, h, device = (
            (xo, 0, right), (xo, 1, left), (xr, 1, right), (xl, 0, left), (xr, 0, right), (xl, 1, left),
        )[kind]
        return remote(acc.at[i, where, h], xrecv.at[i, kind], px_sem, (kind, i), device)

    def pz_copy(i):
        return remote(acc.at[i, x], zrecv.at[z], pz_sem, (i,), at_z(z_step(i)))

    def pieces(i, p, col):
        return gath[i, p, :, :, col : col + feat].reshape(chunk, feat)

    def w_cols(p):
        return w2[:, pl.ds(pl.multiple_of(p * feat, feat), feat)]

    def w_rows(p):
        return w1[pl.ds(pl.multiple_of(p * feat, feat), feat), :]

    def compute(i):
        width = w1.shape[1]
        hidden = jnp.zeros((chunk, width), F32)
        for p in range(NP):
            hidden += jnp.dot(
                pieces(i, p, 0), w1[p * feat : (p + 1) * feat, :], preferred_element_type=F32
            )
        value, slope = gelu_pair(hidden)
        act[i] = value.astype(BF)
        back = jnp.zeros((chunk, width), F32)
        for p in range(NP):
            back += nt_dot(pieces(i, p, feat), w2[:, p * feat : (p + 1) * feat])
        hgrad[i] = (back * slope).astype(BF)
        for q in range(NX):
            p = q * NC + 1 - c
            out = jnp.dot(act[i], w_cols(p), preferred_element_type=F32)
            part[i, q, :, :, :feat] = out.astype(BF).reshape(2, half, feat)
            out = nt_dot(hgrad[i], w_rows(p))
            part[i, q, :, :, feat:] = out.astype(BF).reshape(2, half, feat)

    def own_part(i):
        for q in range(NX):
            p = q * NC + c
            out = jnp.dot(act[i], w_cols(p), preferred_element_type=F32).reshape(2, half, feat)
            out += srecv[i, q, :, :, :feat].astype(F32)
            acc[i, q, :, :, :feat] = out.astype(BF)
            out = nt_dot(hgrad[i], w_rows(p)).reshape(2, half, feat)
            out += srecv[i, q, :, :, feat:].astype(F32)
            acc[i, q, :, :, feat:] = out.astype(BF)

    def add_to(i, where, h, kinds):
        for col in (0, feat):
            total = acc[i, where, h, :, col : col + feat].astype(F32)
            for kind in kinds:
                total += xrecv[i, kind, :, col : col + feat].astype(F32)
            acc[i, where, h, :, col : col + feat] = total.astype(BF)

    def grads(p):
        hg_t = jnp.transpose(hgrad[...].reshape(NZ * chunk, -1).astype(F32)).astype(BF)
        act_t = jnp.transpose(act[...].reshape(NZ * chunk, -1).astype(F32)).astype(BF)
        xs = gath[:, p, :, :, :feat].reshape(NZ * chunk, feat)
        gs = gath[:, p, :, :, feat:].reshape(NZ * chunk, feat)
        first = jnp.dot(hg_t, xs, preferred_element_type=F32)
        gi[p] = jnp.transpose(first).astype(BF)
        go[p] = jnp.dot(act_t, gs, preferred_element_type=F32).astype(BF)

    def gi_copy(p):
        start = pl.multiple_of(p * feat, feat)
        return pltpu.make_async_copy(gi.at[p], grad_in.at[pl.ds(start, feat), :], g_sem.at[0, p])

    def go_copy(p):
        start = pl.multiple_of(p * feat, feat)
        return pltpu.make_async_copy(go.at[p], grad_out.at[:, pl.ds(start, feat)], g_sem.at[1, p])

    load1.wait()
    load2.wait()

    def stage(t, after):
        return (t >= after) & (t < NZ + after)

    @pl.loop(0, NZ + 6)
    def _(t):
        @pl.when((t >= 1) & (t < NZ))
        def _():
            z_copy(t).wait_recv()

        @pl.when(stage(t, 0))
        def _():
            g_copy(0, t).start()
            g_copy(1, t).start()
            s_copy(0, t).start()

        @pl.when(stage(t, 1))
        def _():
            i = t - 1
            g_copy(0, i).wait_recv()
            g_copy(2, i).start()
            s_copy(1, i).start()
            g_copy(1, i).wait_recv()
            g_copy(3, i).start()
            s_copy(2, i).start()

        @pl.when(stage(t, 2))
        def _():
            i = t - 2
            g_copy(2, i).wait_recv()
            g_copy(3, i).wait_recv()
            s_copy(3, i).start()

        @pl.when(stage(t, 5))
        def _():
            i = t - 5
            p_copy(0, i).wait_recv()
            add_to(i, xr, 0, (0,))
            p_copy(4, i).start()
            p_copy(1, i).wait_recv()
            add_to(i, xl, 1, (1,))
            p_copy(5, i).start()

        @pl.when(stage(t, 4))
        def _():
            i = t - 4
            ps_copy(i).wait_recv()
            own_part(i)
            for kind in range(4):
                p_copy(kind, i).start()

        @pl.when(stage(t, 3))
        def _():
            i = t - 3
            for kind in range(4):
                s_copy(kind, i).wait_recv()
            compute(i)
            ps_copy(i).start()

        @pl.when(stage(t, 6))
        def _():
            i = t - 6
            for kind in range(2, 6):
                p_copy(kind, i).wait_recv()
            add_to(i, x, 0, (3, 4))
            add_to(i, x, 1, (2, 5))

            @pl.when(i > 0)
            def _():
                pz_copy(i).start()

            @pl.when(i == 0)
            def _():
                zrecv[z] = acc[0, x]

        @pl.when(t >= NZ + 3)
        def _():
            for k in range(3):
                p = (t - NZ - 3) * 3 + k

                @pl.when(p < NP)
                def _():
                    grads(p)
                    gi_copy(p).start()
                    go_copy(p).start()

    @pl.loop(1, NZ)
    def _(i):
        pz_copy(i).wait_recv()

    for col in (0, feat):
        sums = []
        for h in range(2):
            total = zrecv[h * half_z, :, :, col : col + feat].astype(F32)
            for k in range(1, half_z):
                total += zrecv[h * half_z + k, :, :, col : col + feat].astype(F32)
            sums.append(total.reshape(chunk, feat))
        for k in range(NY):
            block = jnp.concatenate([s[k * cap : (k + 1) * cap] for s in sums], axis=0)
            ysend[k, :, col : col + feat] = block.astype(BF)

    def yb_copy(k):
        return remote(ysend.at[k], yback.at[y], py_sem, (k,), at_y(NY - k))

    for k in range(1, NY):
        yb_copy(k).start()
    yback[y] = ysend[0]
    for k in range(1, NY):
        yb_copy(k).wait_recv()
    home = yback[...].reshape(cells, 2 * feat)
    ffn[...] = jnp.dot(place, home[:, :feat], preferred_element_type=F32).astype(BF)
    gtok[...] = jnp.dot(place, home[:, feat:], preferred_element_type=F32).astype(BF)

    for k in range(1, NY):
        y_copy(k).wait_send()
        yb_copy(k).wait_send()

    @pl.loop(1, NZ)
    def _(i):
        z_copy(i).wait_send()
        pz_copy(i).wait_send()

    @pl.loop(0, NZ)
    def _(i):
        for kind in range(4):
            g_copy(kind, i).wait_send()
            s_copy(kind, i).wait_send()
        ps_copy(i).wait_send()
        for kind in range(6):
            p_copy(kind, i).wait_send()

    @pl.loop(0, NP)
    def _(p):
        gi_copy(p).wait()
        go_copy(p).wait()


def shards(tokens, cotangent, language, owner, w_in, w_out):
    rows, feat = tokens.shape
    depth, width = w_in.shape
    langs = owner.shape[0]
    cap = 3 * rows // (2 * langs)
    chunk = NY * cap
    half = chunk // 2
    vmem, hbm = pl.BlockSpec(memory_space=pltpu.VMEM), pl.BlockSpec(memory_space=pl.ANY)
    dma = pltpu.SemaphoreType.DMA
    return pl.pallas_call(
        kernel,
        out_shape=(
            jax.ShapeDtypeStruct((rows, feat), BF),
            jax.ShapeDtypeStruct((rows, feat), BF),
            jax.ShapeDtypeStruct((depth, width), BF),
            jax.ShapeDtypeStruct((width, depth), BF),
        ),
        in_specs=[vmem] * 4 + [hbm] * 2,
        out_specs=(vmem, vmem, hbm, hbm),
        scratch_shapes=[
            pltpu.VMEM((depth, width), BF),
            pltpu.VMEM((width, depth), BF),
            pltpu.VMEM((NY, 2 * cap, 2 * feat), BF),
            pltpu.VMEM((NY, 2 * cap, 2 * feat), BF),
            pltpu.VMEM((2, 2, half, 2 * feat), BF),
            pltpu.VMEM((NZ, NP, 2, half, 2 * feat), BF),
            pltpu.VMEM((NZ, chunk, width), BF),
            pltpu.VMEM((NZ, chunk, width), BF),
            pltpu.VMEM((NZ, NX, 2, half, 2 * feat), BF),
            pltpu.VMEM((NZ, NX, 2, half, 2 * feat), BF),
            pltpu.VMEM((NZ, NX, 2, half, 2 * feat), BF),
            pltpu.VMEM((NZ, 6, half, 2 * feat), BF),
            pltpu.VMEM((NZ, 2, half, 2 * feat), BF),
            pltpu.VMEM((NY, 2 * cap, 2 * feat), BF),
            pltpu.VMEM((NY, 2 * cap, 2 * feat), BF),
            pltpu.VMEM((NP, feat, width), BF),
            pltpu.VMEM((NP, width, feat), BF),
            dma((2,)),
            dma((2, NP)),
            dma((2, NY)),
            dma((2, NZ)),
            dma((2, 4, NZ)),
            dma((2, 4, NZ)),
            dma((2, NZ)),
            dma((2, 6, NZ)),
            dma((2, NZ)),
            dma((2, NY)),
        ],
        compiler_params=pltpu.CompilerParams(
            collective_id=0, has_side_effects=True, vmem_limit_bytes=60 * 1024 * 1024
        ),
        cost_estimate=pl.CostEstimate(
            flops=12 * NZ * chunk * depth * width, bytes_accessed=16 * depth * width, transcendentals=0
        ),
    )(tokens, cotangent, language, owner.reshape(1, langs), w_in, w_out)


def solution(mesh):
    placed = (
        P("dp", "mp"),
        P("dp", "mp"),
        P("dp", None),
        P(),
        P(None, ("dp", "mp")),
        P(("dp", "mp"), None),
    )
    return jax.shard_map(
        shards,
        mesh=mesh,
        in_specs=placed,
        out_specs=(P("dp", "mp"), P("dp", "mp"), P(None, ("dp", "mp")), P(("dp", "mp"), None)),
        check_vma=False,
    )
```

```python
import jax
import jax.numpy as jnp
from jax import lax
from jax.experimental import pallas as pl
from jax.experimental.pallas import tpu as pltpu
from jax.sharding import PartitionSpec as P

MESH = pl.DeviceIdType.MESH
ROOT_HALF = 0.7071067811865476
INV_ROOT_TAU = 0.3989422804014327

NY, NZ, NX, NC = 4, 8, 4, 2
NP = NX * NC
BF = jnp.bfloat16
F32 = jnp.float32


def gelu_pair(hidden):
    normal_cdf = 0.5 * (1.0 + lax.erf(hidden * ROOT_HALF))
    return (
        hidden * normal_cdf,
        normal_cdf + hidden * jnp.exp(-0.5 * hidden * hidden) * INV_ROOT_TAU,
    )


def back_order(e):
    order = (4, 3, 7, 6, 5, 2, 1, 0)
    return sum(i * ((e - k + 8) // 8) * ((k - e + 8) // 8) for k, i in enumerate(order))


def nt_dot(a, b):
    return lax.dot_general(a, b, (((1,), (1,)), ((), ())), preferred_element_type=F32)


def kernel(
    tok, cot, lang, owner, w_in, w_out,
    ffn, gtok, grad_in, grad_out,
    w1, w2, pack, yrecv, zsend, gath, act, hgrad, part, srecv, acc, xrecv, frecv, qrecv, zrecv,
    ysend, yback, gi, go,
    w_sem, g_sem, y_sem, z_sem, f_sem, q_sem, x_sem, s_sem, ps_sem, px_sem, fr_sem, qr_sem, pz_sem,
    py_sem,
):
    dp, mp = lax.axis_index("dp"), lax.axis_index("mp")
    y, z = dp // NZ, dp % NZ
    x, c = mp // NC, mp % NC
    rows, feat = tok.shape
    cell_rows = pack.shape[1]
    cap = cell_rows // 2
    chunk = NY * cap
    half = chunk // 2
    xr, xl, xo = (x + 1) % NX, (x + NX - 1) % NX, (x + 2) % NX
    sib = {"dp": dp, "mp": x * NC + 1 - c}
    right = {"dp": dp, "mp": xr * NC + c}
    left = {"dp": dp, "mp": xl * NC + c}
    ez = 1 - 2 * (z % 2)

    def at_y(k):
        return {"dp": ((y + k) % NY) * NZ + z, "mp": mp}

    def at_z(k):
        return {"dp": y * NZ + (z + k + NZ) % NZ, "mp": mp}

    def remote(src, dst, sems, where, device):
        return pltpu.make_async_remote_copy(
            src_ref=src,
            dst_ref=dst,
            send_sem=sems.at[(0, *where)],
            recv_sem=sems.at[(1, *where)],
            device_id=device,
            device_id_type=MESH,
        )

    load1 = pltpu.make_async_copy(w_in, w1, w_sem.at[0])
    load2 = pltpu.make_async_copy(w_out, w2, w_sem.at[1])
    load1.start()
    load2.start()

    barrier = pltpu.get_barrier_semaphore()
    partners = [sib, right, left] + [at_y(k) for k in range(1, NY)]
    partners += [at_z(k * ez) for k in (1, -1, 2, -2, -3)]
    for device in partners:
        pl.semaphore_signal(barrier, inc=1, device_id=device, device_id_type=MESH)

    langs = owner.shape[1]
    hit = lang[...] == lax.broadcasted_iota(jnp.int32, (langs, rows), 0)
    upper = (
        lax.broadcasted_iota(jnp.int32, (rows, rows), 0)
        < lax.broadcasted_iota(jnp.int32, (rows, rows), 1)
    )
    before = jnp.dot(
        jnp.where(hit, 1.0, 0.0).astype(BF),
        jnp.where(upper, 1.0, 0.0).astype(BF),
        preferred_element_type=F32,
    )
    diagonal = lax.broadcasted_iota(jnp.int32, (langs, langs), 0) == lax.broadcasted_iota(
        jnp.int32, (langs, langs), 1
    )
    slots = jnp.sum(jnp.where(diagonal, owner[...].astype(F32), 0.0), axis=1, keepdims=True)
    cell = jnp.sum(jnp.where(hit, before + slots * cap, 0.0), axis=0, keepdims=True)
    cells = langs * cap
    place_t = jnp.where(
        cell.astype(jnp.int32) == lax.broadcasted_iota(jnp.int32, (cells, rows), 0), 1.0, 0.0
    )
    place = jnp.transpose(place_t).astype(BF)
    place_t = place_t.astype(BF)
    packed_x = jnp.dot(place_t, tok[...], preferred_element_type=F32).astype(BF)
    packed_g = jnp.dot(place_t, cot[...], preferred_element_type=F32).astype(BF)
    pack[:, :, :feat] = packed_x.reshape(NY, cell_rows, feat)
    pack[:, :, feat:] = packed_g.reshape(NY, cell_rows, feat)

    pl.semaphore_wait(barrier, len(partners))

    def y_copy(k):
        return remote(pack.at[(y + k) % NY], yrecv.at[k], y_sem, (k,), at_y(k))

    for k in range(1, NY):
        y_copy(k).start()
    yrecv[0] = pack[y]
    for k in range(1, NY):
        y_copy(k).wait_recv()
    for h in range(2):
        for col in (0, feat):
            block = jnp.concatenate(
                [
                    yrecv[k, :, col : col + feat].astype(F32)[h * cap : (h + 1) * cap]
                    for k in range(NY)
                ],
                axis=0,
            ).astype(BF)
            zsend[h, :, :, col : col + feat] = block.reshape(2, half, feat)

    half_z = NZ // 2
    pair = at_z(ez)

    def z_copy(k):
        to = (z + (0, -ez, 2 * ez, -3 * ez)[k] + NZ) % NZ
        device = {"dp": y * NZ + to, "mp": mp}
        return remote(zsend.at[to // half_z], gath.at[2 * k - 1, mp], z_sem, (k,), device)

    def z_arrived(k):
        return remote(zsend.at[0], gath.at[2 * k - 1, mp], z_sem, (k,), pair)

    def f_copy(k):
        return remote(gath.at[2 * k - 1, mp], gath.at[2 * k, mp], f_sem, (k,), pair)

    def q_copy(kind):
        p = (x, xl, xr, xo)[kind] * NC + c
        return remote(gath.at[0, p], gath.at[NZ - 1, p], q_sem, (kind,), pair)

    z_copy(1).start()
    gath[0, mp] = zsend[z // half_z]

    def g_copy(kind, i):
        if kind == 0:
            return remote(gath.at[i, mp], gath.at[i, mp], x_sem, (0, i), right)
        if kind == 1:
            return remote(gath.at[i, mp], gath.at[i, mp], x_sem, (1, i), left)
        if kind == 2:
            src = gath.at[i, xl * NC + c, 0]
            return remote(src, src, x_sem, (2, i), right)
        src = gath.at[i, xr * NC + c, 1]
        return remote(src, src, x_sem, (3, i), left)

    def s_copy(kind, i):
        src = gath.at[i, (x, xl, xr, xo)[kind] * NC + c]
        return remote(src, src, s_sem, (kind, i), sib)

    def ps_copy(i):
        return remote(part.at[i], srecv.at[i], ps_sem, (i,), sib)

    def p_copy(kind, i):
        where, h, device = (
            (xo, 0, right), (xo, 1, left), (xr, 1, right), (xl, 0, left), (xr, 0, right), (xl, 1, left),
        )[kind]
        return remote(acc.at[i, where, h], xrecv.at[i, kind], px_sem, (kind, i), device)

    def fr_copy(k):
        return remote(acc.at[2 * k, x], frecv.at[k], fr_sem, (k,), pair)

    def qr_copy(q):
        return remote(acc.at[NZ - 1, q], qrecv.at[q], qr_sem, (q,), pair)

    def pz_copy(k):
        return remote(acc.at[2 * k - 1, x], zrecv.at[z // 2], pz_sem, (k,), at_z(-k * ez))

    def pieces(i, p, col):
        return gath[i, p, :, :, col : col + feat].reshape(chunk, feat)

    def w_cols(p):
        return w2[:, pl.ds(pl.multiple_of(p * feat, feat), feat)]

    def w_rows(p):
        return w1[pl.ds(pl.multiple_of(p * feat, feat), feat), :]

    def compute(i):
        width = w1.shape[1]
        hidden = jnp.zeros((chunk, width), F32)
        for p in range(NP):
            hidden += jnp.dot(
                pieces(i, p, 0), w1[p * feat : (p + 1) * feat, :], preferred_element_type=F32
            )
        value, slope = gelu_pair(hidden)
        act[i] = value.astype(BF)
        back = jnp.zeros((chunk, width), F32)
        for p in range(NP):
            back += nt_dot(pieces(i, p, feat), w2[:, p * feat : (p + 1) * feat])
        hgrad[i] = (back * slope).astype(BF)

    def sib_part(i):
        for q in range(NX):
            p = q * NC + 1 - c
            out = jnp.dot(act[i], w_cols(p), preferred_element_type=F32)
            part[i, q, :, :, :feat] = out.astype(BF).reshape(2, half, feat)
            out = nt_dot(hgrad[i], w_rows(p))
            part[i, q, :, :, feat:] = out.astype(BF).reshape(2, half, feat)

    def own_part(i):
        for q in range(NX):
            p = q * NC + c
            out = jnp.dot(act[i], w_cols(p), preferred_element_type=F32).reshape(2, half, feat)
            out += srecv[i, q, :, :, :feat].astype(F32)
            acc[i, q, :, :, :feat] = out.astype(BF)
            out = nt_dot(hgrad[i], w_rows(p)).reshape(2, half, feat)
            out += srecv[i, q, :, :, feat:].astype(F32)
            acc[i, q, :, :, feat:] = out.astype(BF)

    def add_pair(i, q, ref):
        for h in range(2):
            for col in (0, feat):
                total = acc[i, q, h, :, col : col + feat].astype(F32)
                total += ref[h, :, col : col + feat].astype(F32)
                acc[i, q, h, :, col : col + feat] = total.astype(BF)

    def add_to(i, where, h, kinds):
        for col in (0, feat):
            total = acc[i, where, h, :, col : col + feat].astype(F32)
            for kind in kinds:
                total += xrecv[i, kind, :, col : col + feat].astype(F32)
            acc[i, where, h, :, col : col + feat] = total.astype(BF)

    def grads(p):
        hg_t = jnp.transpose(hgrad[...].reshape(NZ * chunk, -1).astype(F32)).astype(BF)
        act_t = jnp.transpose(act[...].reshape(NZ * chunk, -1).astype(F32)).astype(BF)
        xs = gath[:, p, :, :, :feat].reshape(NZ * chunk, feat)
        gs = gath[:, p, :, :, feat:].reshape(NZ * chunk, feat)
        first = jnp.dot(hg_t, xs, preferred_element_type=F32)
        gi[p] = jnp.transpose(first).astype(BF)
        go[p] = jnp.dot(act_t, gs, preferred_element_type=F32).astype(BF)

    def gi_copy(p):
        start = pl.multiple_of(p * feat, feat)
        return pltpu.make_async_copy(gi.at[p], grad_in.at[pl.ds(start, feat), :], g_sem.at[0, p])

    def go_copy(p):
        start = pl.multiple_of(p * feat, feat)
        return pltpu.make_async_copy(go.at[p], grad_out.at[:, pl.ds(start, feat)], g_sem.at[1, p])

    load1.wait()
    load2.wait()

    def stage(t, after, count=NZ):
        return (t >= after) & (t < count + after)

    last = NZ - 1
    first_back = NZ - 1

    @pl.loop(0, NZ + first_back + 3)
    def _(t):
        @pl.when((t >= 2) & (t < last) & (t % 2 == 0))
        def _():
            f_copy(t // 2).wait_recv()

        @pl.when(stage(t, 0, last))
        def _():
            g_copy(0, t).start()
            g_copy(1, t).start()
            s_copy(0, t).start()

        @pl.when((t < last - 1) & (t % 2 == 0))
        def _():
            k = t // 2 + 1
            z_arrived(k).wait_recv()
            f_copy(k).start()

        for k in (1, 2):

            @pl.when(t == 2 * k - 2)
            def _():
                z_copy(k + 1).start()

        @pl.when(stage(t, 1, last))
        def _():
            i = t - 1
            g_copy(0, i).wait_recv()
            g_copy(2, i).start()
            s_copy(1, i).start()
            g_copy(1, i).wait_recv()
            g_copy(3, i).start()
            s_copy(2, i).start()

        @pl.when(stage(t, 2, last))
        def _():
            i = t - 2
            g_copy(2, i).wait_recv()
            g_copy(3, i).wait_recv()
            s_copy(3, i).start()

        for kind in range(4):

            @pl.when(t == 3 + kind)
            def _():
                q_copy(kind).start()

        @pl.when(t == last + 1)
        def _():
            for kind in range(4):
                q_copy(kind).wait_recv()
                s_copy(kind, last).start()

        @pl.when(stage(t, first_back + 4))
        def _():
            i = back_order(t - first_back - 4)

            @pl.when((i < last) & (i % 2 == 1))
            def _():
                k = (i + 1) // 2
                fr_copy(k).wait_recv()
                add_pair(i, x, frecv.at[k])
                pz_copy(k).start()

        @pl.when(stage(t, first_back + 1))
        def _():
            i = back_order(t - first_back - 1)
            ps_copy(i).wait_recv()
            own_part(i)

            @pl.when(i == 0)
            def _():
                for q in range(NX):
                    qr_copy(q).wait_recv()
                    add_pair(0, q, qrecv.at[q])

            @pl.when(i < last)
            def _():
                for kind in range(4):
                    p_copy(kind, i).start()

        @pl.when(stage(t, first_back + 2))
        def _():
            i = back_order(t - first_back - 2)

            @pl.when(i < last)
            def _():
                p_copy(0, i).wait_recv()
                add_to(i, xr, 0, (0,))
                p_copy(4, i).start()
                p_copy(1, i).wait_recv()
                add_to(i, xl, 1, (1,))
                p_copy(5, i).start()

        for q in range(NX):

            @pl.when(t == last + 3 + q)
            def _():
                qr_copy(q).start()

        @pl.when(stage(t, 3, last))
        def _():
            i = t - 3
            for kind in range(4):
                s_copy(kind, i).wait_recv()
            compute(i)

        @pl.when(t == last + 2)
        def _():
            for kind in range(4):
                s_copy(kind, last).wait_recv()
            compute(last)

        @pl.when(stage(t, first_back))
        def _():
            i = back_order(t - first_back)
            sib_part(i)
            ps_copy(i).start()

        @pl.when(stage(t, first_back + 3))
        def _():
            i = back_order(t - first_back - 3)

            @pl.when(i < last)
            def _():
                for kind in range(2, 6):
                    p_copy(kind, i).wait_recv()
                add_to(i, x, 0, (3, 4))
                add_to(i, x, 1, (2, 5))

            @pl.when((i > 0) & (i % 2 == 0))
            def _():
                fr_copy(i // 2).start()

            @pl.when(i == 0)
            def _():
                zrecv[z // 2] = acc[0, x]

        @pl.when(stage(t, NZ + 2))
        def _():
            p = t - NZ - 2
            grads(p)
            gi_copy(p).start()
            go_copy(p).start()

    for k in (1, 2, 3):
        pz_copy(k).wait_recv()

    for col in (0, feat):
        sums = []
        for h in range(2):
            total = zrecv[2 * h, :, :, col : col + feat].astype(F32)
            total += zrecv[2 * h + 1, :, :, col : col + feat].astype(F32)
            sums.append(total.reshape(chunk, feat))
        for k in range(NY):
            block = jnp.concatenate([s[k * cap : (k + 1) * cap] for s in sums], axis=0)
            ysend[k, :, col : col + feat] = block.astype(BF)

    def yb_copy(k):
        return remote(ysend.at[k], yback.at[y], py_sem, (k,), at_y(NY - k))

    for k in range(1, NY):
        yb_copy(k).start()
    yback[y] = ysend[0]
    for k in range(1, NY):
        yb_copy(k).wait_recv()
    home = yback[...].reshape(cells, 2 * feat)
    ffn[...] = jnp.dot(place, home[:, :feat], preferred_element_type=F32).astype(BF)
    gtok[...] = jnp.dot(place, home[:, feat:], preferred_element_type=F32).astype(BF)

    for k in range(1, NY):
        y_copy(k).wait_send()
        yb_copy(k).wait_send()

        z_copy(k).wait_send()
        f_copy(k).wait_send()
        fr_copy(k).wait_send()
        pz_copy(k).wait_send()
    for kind in range(4):
        q_copy(kind).wait_send()
    for q in range(NX):
        qr_copy(q).wait_send()

    @pl.loop(0, NZ)
    def _(i):
        for kind in range(4):
            s_copy(kind, i).wait_send()
        ps_copy(i).wait_send()

    @pl.loop(0, last)
    def _(i):
        for kind in range(4):
            g_copy(kind, i).wait_send()
        for kind in range(6):
            p_copy(kind, i).wait_send()

    @pl.loop(0, NP)
    def _(p):
        gi_copy(p).wait()
        go_copy(p).wait()


def hand_over(a0, a1, a2, a3, b0, b1, b2, b3, v0, v1, v2, v3, sems):
    moves = []
    for k, (src, mid, dst) in enumerate(((a2, v2, b2), (a3, v3, b3), (a0, v0, b0), (a1, v1, b1))):
        parts = 4 if k < 2 else 1
        size = src.shape[0] // parts
        for n in range(parts):
            rows = pl.ds(n * size, size)
            moves.append(
                (
                    pltpu.make_async_copy(src.at[rows], mid.at[rows], sems.at[0, k, n]),
                    pltpu.make_async_copy(mid.at[rows], dst.at[rows], sems.at[1, k, n]),
                )
            )
    for first, _ in moves:
        first.start()
    for first, second in moves:
        first.wait()
        second.start()
    for _, second in moves:
        second.wait()


def shards(tokens, cotangent, language, owner, w_in, w_out):
    rows, feat = tokens.shape
    depth, width = w_in.shape
    langs = owner.shape[0]
    cap = 3 * rows // (2 * langs)
    chunk = NY * cap
    half = chunk // 2
    vmem, hbm = pl.BlockSpec(memory_space=pltpu.VMEM), pl.BlockSpec(memory_space=pl.ANY)
    dma = pltpu.SemaphoreType.DMA
    results = pl.pallas_call(
        kernel,
        out_shape=(
            jax.ShapeDtypeStruct((rows, feat), BF),
            jax.ShapeDtypeStruct((rows, feat), BF),
            jax.ShapeDtypeStruct((depth, width), BF),
            jax.ShapeDtypeStruct((width, depth), BF),
        ),
        in_specs=[vmem] * 4 + [hbm] * 2,
        out_specs=(vmem, vmem, hbm, hbm),
        scratch_shapes=[
            pltpu.VMEM((depth, width), BF),
            pltpu.VMEM((width, depth), BF),
            pltpu.VMEM((NY, 2 * cap, 2 * feat), BF),
            pltpu.VMEM((NY, 2 * cap, 2 * feat), BF),
            pltpu.VMEM((2, 2, half, 2 * feat), BF),
            pltpu.VMEM((NZ, NP, 2, half, 2 * feat), BF),
            pltpu.VMEM((NZ, chunk, width), BF),
            pltpu.VMEM((NZ, chunk, width), BF),
            pltpu.VMEM((NZ, NX, 2, half, 2 * feat), BF),
            pltpu.VMEM((NZ, NX, 2, half, 2 * feat), BF),
            pltpu.VMEM((NZ, NX, 2, half, 2 * feat), BF),
            pltpu.VMEM((NZ, 6, half, 2 * feat), BF),
            pltpu.VMEM((4, 2, half, 2 * feat), BF),
            pltpu.VMEM((NX, 2, half, 2 * feat), BF),
            pltpu.VMEM((NZ // 2, 2, half, 2 * feat), BF),
            pltpu.VMEM((NY, 2 * cap, 2 * feat), BF),
            pltpu.VMEM((NY, 2 * cap, 2 * feat), BF),
            pltpu.VMEM((NP, feat, width), BF),
            pltpu.VMEM((NP, width, feat), BF),
            dma((2,)),
            dma((2, NP)),
            dma((2, NY)),
            dma((2, 4)),
            dma((2, 4)),
            dma((2, 4)),
            dma((2, 4, NZ)),
            dma((2, 4, NZ)),
            dma((2, NZ)),
            dma((2, 6, NZ)),
            dma((2, 4)),
            dma((2, NX)),
            dma((2, 4)),
            dma((2, NY)),
        ],
        compiler_params=pltpu.CompilerParams(
            collective_id=0, has_side_effects=True, vmem_limit_bytes=60 * 1024 * 1024
        ),
        cost_estimate=pl.CostEstimate(
            flops=12 * NZ * chunk * depth * width, bytes_accessed=16 * depth * width, transcendentals=0
        ),
    )(tokens, cotangent, language.reshape(1, rows), owner.reshape(1, langs), w_in, w_out)
    return pl.pallas_call(
        hand_over,
        out_shape=tuple(jax.ShapeDtypeStruct(r.shape, r.dtype) for r in results),
        in_specs=[hbm] * 4,
        out_specs=(hbm,) * 4,
        scratch_shapes=[pltpu.VMEM(r.shape, r.dtype) for r in results] + [dma((2, 4, 4))],
        compiler_params=pltpu.CompilerParams(vmem_limit_bytes=60 * 1024 * 1024),
    )(*results)


def solution(mesh):
    placed = (
        P("dp", "mp"),
        P("dp", "mp"),
        P("dp", None),
        P(),
        P(None, ("dp", "mp")),
        P(("dp", "mp"), None),
    )
    return jax.shard_map(
        shards,
        mesh=mesh,
        in_specs=placed,
        out_specs=(P("dp", "mp"), P("dp", "mp"), P(None, ("dp", "mp")), P(("dp", "mp"), None)),
        check_vma=False,
    )
```

```python
import jax
import jax.numpy as jnp
from jax import lax
from jax.experimental import pallas as pl
from jax.experimental.pallas import tpu as pltpu
from jax.sharding import PartitionSpec as P

MESH = pl.DeviceIdType.MESH
ROOT_HALF = 0.7071067811865476
INV_ROOT_TAU = 0.3989422804014327

NY, NZ, NX, NC = 4, 8, 4, 2
NP = NX * NC
BF = jnp.bfloat16
F32 = jnp.float32


def gelu_pair(hidden):
    normal_cdf = 0.5 * (1.0 + lax.erf(hidden * ROOT_HALF))
    return (
        hidden * normal_cdf,
        normal_cdf + hidden * jnp.exp(-0.5 * hidden * hidden) * INV_ROOT_TAU,
    )


def back_order(e):
    order = (4, 7, 3, 6, 5, 2, 1, 0)
    return sum(i * ((e - k + 8) // 8) * ((k - e + 8) // 8) for k, i in enumerate(order))


def nt_dot(a, b):
    return lax.dot_general(a, b, (((1,), (1,)), ((), ())), preferred_element_type=F32)


def kernel(
    tok, cot, lang, owner, w_in, w_out,
    ffn, gtok, grad_in, grad_out,
    w1, w2, pack, yrecv, zsend, gath, act, hgrad, part, srecv, acc, xrecv, frecv, qrecv, zrecv,
    ysend, yback, gi, go,
    w_sem, g_sem, y_sem, z_sem, f_sem, q_sem, x_sem, s_sem, ps_sem, px_sem, fr_sem, qr_sem, pz_sem,
    py_sem,
):
    dp, mp = lax.axis_index("dp"), lax.axis_index("mp")
    y, z = dp // NZ, dp % NZ
    x, c = mp // NC, mp % NC
    rows, feat = tok.shape
    cell_rows = pack.shape[1]
    cap = cell_rows // 2
    chunk = NY * cap
    half = chunk // 2
    xr, xl, xo = (x + 1) % NX, (x + NX - 1) % NX, (x + 2) % NX
    sib = {"dp": dp, "mp": x * NC + 1 - c}
    right = {"dp": dp, "mp": xr * NC + c}
    left = {"dp": dp, "mp": xl * NC + c}
    ez = 1 - 2 * (z % 2)

    def at_y(k):
        return {"dp": ((y + k) % NY) * NZ + z, "mp": mp}

    def at_z(k):
        return {"dp": y * NZ + (z + k + NZ) % NZ, "mp": mp}

    def remote(src, dst, sems, where, device):
        return pltpu.make_async_remote_copy(
            src_ref=src,
            dst_ref=dst,
            send_sem=sems.at[(0, *where)],
            recv_sem=sems.at[(1, *where)],
            device_id=device,
            device_id_type=MESH,
        )

    load1 = pltpu.make_async_copy(w_in, w1, w_sem.at[0])
    load2 = pltpu.make_async_copy(w_out, w2, w_sem.at[1])
    load1.start()
    load2.start()

    barrier = pltpu.get_barrier_semaphore()
    partners = [sib, right, left] + [at_y(k) for k in range(1, NY)]
    partners += [at_z(k * ez) for k in (1, -1, 2, -2, -3)]
    for device in partners:
        pl.semaphore_signal(barrier, inc=1, device_id=device, device_id_type=MESH)

    langs = owner.shape[1]
    hit = lang[...] == lax.broadcasted_iota(jnp.int32, (langs, rows), 0)
    upper = (
        lax.broadcasted_iota(jnp.int32, (rows, rows), 0)
        < lax.broadcasted_iota(jnp.int32, (rows, rows), 1)
    )
    before = jnp.dot(
        jnp.where(hit, 1.0, 0.0).astype(BF),
        jnp.where(upper, 1.0, 0.0).astype(BF),
        preferred_element_type=F32,
    )
    diagonal = lax.broadcasted_iota(jnp.int32, (langs, langs), 0) == lax.broadcasted_iota(
        jnp.int32, (langs, langs), 1
    )
    slots = jnp.sum(jnp.where(diagonal, owner[...].astype(F32), 0.0), axis=1, keepdims=True)
    cell = jnp.sum(jnp.where(hit, before + slots * cap, 0.0), axis=0, keepdims=True)
    cells = langs * cap
    place_t = jnp.where(
        cell.astype(jnp.int32) == lax.broadcasted_iota(jnp.int32, (cells, rows), 0), 1.0, 0.0
    )
    place = jnp.transpose(place_t).astype(BF)
    place_t = place_t.astype(BF)
    packed_x = jnp.dot(place_t, tok[...], preferred_element_type=F32).astype(BF)
    packed_g = jnp.dot(place_t, cot[...], preferred_element_type=F32).astype(BF)
    pack[:, :, :feat] = packed_x.reshape(NY, cell_rows, feat)
    pack[:, :, feat:] = packed_g.reshape(NY, cell_rows, feat)

    pl.semaphore_wait(barrier, len(partners))

    def y_copy(k):
        return remote(pack.at[(y + k) % NY], yrecv.at[k], y_sem, (k,), at_y(k))

    for k in range(1, NY):
        y_copy(k).start()
    yrecv[0] = pack[y]
    for k in range(1, NY):
        y_copy(k).wait_recv()
    for h in range(2):
        for col in (0, feat):
            block = jnp.concatenate(
                [
                    yrecv[k, :, col : col + feat].astype(F32)[h * cap : (h + 1) * cap]
                    for k in range(NY)
                ],
                axis=0,
            ).astype(BF)
            zsend[h, :, :, col : col + feat] = block.reshape(2, half, feat)

    half_z = NZ // 2
    pair = at_z(ez)

    def z_copy(k):
        to = (z + (0, -ez, 2 * ez, -3 * ez)[k] + NZ) % NZ
        device = {"dp": y * NZ + to, "mp": mp}
        return remote(zsend.at[to // half_z], gath.at[2 * k - 1, mp], z_sem, (k,), device)

    def z_arrived(k):
        return remote(zsend.at[0], gath.at[2 * k - 1, mp], z_sem, (k,), pair)

    def f_copy(k):
        return remote(gath.at[2 * k - 1, mp], gath.at[2 * k, mp], f_sem, (k,), pair)

    def q_copy(kind):
        p = (x, xl, xr, xo)[kind] * NC + c
        return remote(gath.at[0, p], gath.at[NZ - 1, p], q_sem, (kind,), pair)

    z_copy(1).start()
    gath[0, mp] = zsend[z // half_z]

    def g_copy(kind, i):
        if kind == 0:
            return remote(gath.at[i, mp], gath.at[i, mp], x_sem, (0, i), right)
        if kind == 1:
            return remote(gath.at[i, mp], gath.at[i, mp], x_sem, (1, i), left)
        if kind == 2:
            src = gath.at[i, xl * NC + c, 0]
            return remote(src, src, x_sem, (2, i), right)
        src = gath.at[i, xr * NC + c, 1]
        return remote(src, src, x_sem, (3, i), left)

    def s_copy(kind, i):
        src = gath.at[i, (x, xl, xr, xo)[kind] * NC + c]
        return remote(src, src, s_sem, (kind, i), sib)

    def ps_copy(i):
        return remote(part.at[i], srecv.at[i], ps_sem, (i,), sib)

    def p_copy(kind, i):
        where, h, device = (
            (xo, 0, right), (xo, 1, left), (xr, 1, right), (xl, 0, left), (xr, 0, right), (xl, 1, left),
        )[kind]
        return remote(acc.at[i, where, h], xrecv.at[i, kind], px_sem, (kind, i), device)

    def fr_copy(k):
        return remote(acc.at[2 * k, x], frecv.at[k], fr_sem, (k,), pair)

    def qr_copy(q):
        return remote(acc.at[NZ - 1, q], qrecv.at[q], qr_sem, (q,), pair)

    def pz_copy(k):
        return remote(acc.at[2 * k - 1, x], zrecv.at[z // 2], pz_sem, (k,), at_z(-k * ez))

    def pieces(i, p, col):
        return gath[i, p, :, :, col : col + feat].reshape(chunk, feat)

    def w_cols(p):
        return w2[:, pl.ds(pl.multiple_of(p * feat, feat), feat)]

    def w_rows(p):
        return w1[pl.ds(pl.multiple_of(p * feat, feat), feat), :]

    def compute(i):
        width = w1.shape[1]
        hidden = jnp.zeros((chunk, width), F32)
        for p in range(NP):
            hidden += jnp.dot(
                pieces(i, p, 0), w1[p * feat : (p + 1) * feat, :], preferred_element_type=F32
            )
        value, slope = gelu_pair(hidden)
        act[i] = value.astype(BF)
        back = jnp.zeros((chunk, width), F32)
        for p in range(NP):
            back += nt_dot(pieces(i, p, feat), w2[:, p * feat : (p + 1) * feat])
        hgrad[i] = (back * slope).astype(BF)

    def sib_part(i):
        for q in range(NX):
            p = q * NC + 1 - c
            out = jnp.dot(act[i], w_cols(p), preferred_element_type=F32)
            part[i, q, :, :, :feat] = out.astype(BF).reshape(2, half, feat)
            out = nt_dot(hgrad[i], w_rows(p))
            part[i, q, :, :, feat:] = out.astype(BF).reshape(2, half, feat)

    def own_part(i):
        for q in range(NX):
            p = q * NC + c
            out = jnp.dot(act[i], w_cols(p), preferred_element_type=F32).reshape(2, half, feat)
            out += srecv[i, q, :, :, :feat].astype(F32)
            acc[i, q, :, :, :feat] = out.astype(BF)
            out = nt_dot(hgrad[i], w_rows(p)).reshape(2, half, feat)
            out += srecv[i, q, :, :, feat:].astype(F32)
            acc[i, q, :, :, feat:] = out.astype(BF)

    def add_pair(i, q, ref):
        for h in range(2):
            for col in (0, feat):
                total = acc[i, q, h, :, col : col + feat].astype(F32)
                total += ref[h, :, col : col + feat].astype(F32)
                acc[i, q, h, :, col : col + feat] = total.astype(BF)

    def add_to(i, where, h, kinds):
        for col in (0, feat):
            total = acc[i, where, h, :, col : col + feat].astype(F32)
            for kind in kinds:
                total += xrecv[i, kind, :, col : col + feat].astype(F32)
            acc[i, where, h, :, col : col + feat] = total.astype(BF)

    def grads(p):
        hg_t = jnp.transpose(hgrad[...].reshape(NZ * chunk, -1).astype(F32)).astype(BF)
        act_t = jnp.transpose(act[...].reshape(NZ * chunk, -1).astype(F32)).astype(BF)
        xs = gath[:, p, :, :, :feat].reshape(NZ * chunk, feat)
        gs = gath[:, p, :, :, feat:].reshape(NZ * chunk, feat)
        first = jnp.dot(hg_t, xs, preferred_element_type=F32)
        gi[p] = jnp.transpose(first).astype(BF)
        go[p] = jnp.dot(act_t, gs, preferred_element_type=F32).astype(BF)

    def gi_copy(p):
        start = pl.multiple_of(p * feat, feat)
        return pltpu.make_async_copy(gi.at[p], grad_in.at[pl.ds(start, feat), :], g_sem.at[0, p])

    def go_copy(p):
        start = pl.multiple_of(p * feat, feat)
        return pltpu.make_async_copy(go.at[p], grad_out.at[:, pl.ds(start, feat)], g_sem.at[1, p])

    load1.wait()
    load2.wait()

    def stage(t, after, count=NZ):
        return (t >= after) & (t < count + after)

    last = NZ - 1
    first_back = NZ - 1

    @pl.loop(0, NZ + first_back + 3)
    def _(t):
        @pl.when(stage(t, first_back + 1))
        def _():
            i = back_order(t - first_back - 1)
            ps_copy(i).wait_recv()
            own_part(i)

            @pl.when(i == 0)
            def _():
                for q in range(NX):
                    qr_copy(q).wait_recv()
                    add_pair(0, q, qrecv.at[q])

            @pl.when(i < last)
            def _():
                for kind in range(4):
                    p_copy(kind, i).start()

        @pl.when((t >= 2) & (t < last) & (t % 2 == 0))
        def _():
            f_copy(t // 2).wait_recv()

        @pl.when((t < last) & (t % 2 == 1))
        def _():
            k = (t + 1) // 2
            z_arrived(k).wait_recv()
            f_copy(k).start()

        for k in (2, 3):

            @pl.when(t == k)
            def _():
                z_copy(k).start()

        @pl.when(stage(t, 0, last))
        def _():
            g_copy(0, t).start()
            g_copy(1, t).start()
            s_copy(0, t).start()

        @pl.when(stage(t, 1, last))
        def _():
            i = t - 1
            g_copy(0, i).wait_recv()
            g_copy(2, i).start()
            s_copy(1, i).start()
            g_copy(1, i).wait_recv()
            g_copy(3, i).start()
            s_copy(2, i).start()

        @pl.when(stage(t, 2, last))
        def _():
            i = t - 2
            g_copy(2, i).wait_recv()
            g_copy(3, i).wait_recv()
            s_copy(3, i).start()

        for kind in range(4):

            @pl.when(t == min(3 + kind, 5))
            def _():
                q_copy(kind).start()

        @pl.when(t == last)
        def _():
            for kind in range(4):
                q_copy(kind).wait_recv()
                s_copy(kind, last).start()

        @pl.when(stage(t, first_back + 4))
        def _():
            i = back_order(t - first_back - 4)

            @pl.when((i < last) & (i % 2 == 1))
            def _():
                k = (i + 1) // 2
                fr_copy(k).wait_recv()
                add_pair(i, x, frecv.at[k])
                pz_copy(k).start()

        @pl.when(stage(t, first_back + 2))
        def _():
            i = back_order(t - first_back - 2)

            @pl.when(i < last)
            def _():
                p_copy(0, i).wait_recv()
                add_to(i, xr, 0, (0,))
                p_copy(4, i).start()
                p_copy(1, i).wait_recv()
                add_to(i, xl, 1, (1,))
                p_copy(5, i).start()

        for q in range(NX):

            @pl.when(t == last + 2 + q)
            def _():
                qr_copy(q).start()

        @pl.when(stage(t, 3, last))
        def _():
            i = t - 3
            for kind in range(4):
                s_copy(kind, i).wait_recv()
            compute(i)

        @pl.when(t == last + 1)
        def _():
            for kind in range(4):
                s_copy(kind, last).wait_recv()
            compute(last)

        @pl.when(stage(t, first_back))
        def _():
            i = back_order(t - first_back)
            sib_part(i)
            ps_copy(i).start()

        @pl.when(stage(t, first_back + 3))
        def _():
            i = back_order(t - first_back - 3)

            @pl.when(i < last)
            def _():
                for kind in range(2, 6):
                    p_copy(kind, i).wait_recv()
                add_to(i, x, 0, (3, 4))
                add_to(i, x, 1, (2, 5))

            @pl.when((i > 0) & (i % 2 == 0))
            def _():
                fr_copy(i // 2).start()

            @pl.when(i == 0)
            def _():
                zrecv[z // 2] = acc[0, x]

        @pl.when(stage(t, NZ + 2))
        def _():
            p = t - NZ - 2
            grads(p)
            gi_copy(p).start()
            go_copy(p).start()

    for k in (1, 2, 3):
        pz_copy(k).wait_recv()

    for col in (0, feat):
        sums = []
        for h in range(2):
            total = zrecv[2 * h, :, :, col : col + feat].astype(F32)
            total += zrecv[2 * h + 1, :, :, col : col + feat].astype(F32)
            sums.append(total.reshape(chunk, feat))
        for k in range(NY):
            block = jnp.concatenate([s[k * cap : (k + 1) * cap] for s in sums], axis=0)
            ysend[k, :, col : col + feat] = block.astype(BF)

    def yb_copy(k):
        return remote(ysend.at[k], yback.at[y], py_sem, (k,), at_y(NY - k))

    for k in range(1, NY):
        yb_copy(k).start()
    yback[y] = ysend[0]
    for k in range(1, NY):
        yb_copy(k).wait_recv()
    home = yback[...].reshape(cells, 2 * feat)
    ffn[...] = jnp.dot(place, home[:, :feat], preferred_element_type=F32).astype(BF)
    gtok[...] = jnp.dot(place, home[:, feat:], preferred_element_type=F32).astype(BF)

    for k in range(1, NY):
        y_copy(k).wait_send()
        yb_copy(k).wait_send()

        z_copy(k).wait_send()
        f_copy(k).wait_send()
        fr_copy(k).wait_send()
        pz_copy(k).wait_send()
    for kind in range(4):
        q_copy(kind).wait_send()
    for q in range(NX):
        qr_copy(q).wait_send()

    @pl.loop(0, NZ)
    def _(i):
        for kind in range(4):
            s_copy(kind, i).wait_send()
        ps_copy(i).wait_send()

    @pl.loop(0, last)
    def _(i):
        for kind in range(4):
            g_copy(kind, i).wait_send()
        for kind in range(6):
            p_copy(kind, i).wait_send()

    @pl.loop(0, NP)
    def _(p):
        gi_copy(p).wait()
        go_copy(p).wait()


def hand_over(a0, a1, a2, a3, b0, b1, b2, b3, v0, v1, v2, v3, sems):
    moves = []
    for k, (src, mid, dst) in enumerate(((a2, v2, b2), (a3, v3, b3), (a0, v0, b0), (a1, v1, b1))):
        parts = 4 if k < 2 else 1
        size = src.shape[0] // parts
        for n in range(parts):
            rows = pl.ds(n * size, size)
            moves.append(
                (
                    pltpu.make_async_copy(src.at[rows], mid.at[rows], sems.at[0, k, n]),
                    pltpu.make_async_copy(mid.at[rows], dst.at[rows], sems.at[1, k, n]),
                )
            )
    for first, _ in moves:
        first.start()
    for first, second in moves:
        first.wait()
        second.start()
    for _, second in moves:
        second.wait()


def shards(tokens, cotangent, language, owner, w_in, w_out):
    rows, feat = tokens.shape
    depth, width = w_in.shape
    langs = owner.shape[0]
    cap = 3 * rows // (2 * langs)
    chunk = NY * cap
    half = chunk // 2
    vmem, hbm = pl.BlockSpec(memory_space=pltpu.VMEM), pl.BlockSpec(memory_space=pl.ANY)
    dma = pltpu.SemaphoreType.DMA
    results = pl.pallas_call(
        kernel,
        out_shape=(
            jax.ShapeDtypeStruct((rows, feat), BF),
            jax.ShapeDtypeStruct((rows, feat), BF),
            jax.ShapeDtypeStruct((depth, width), BF),
            jax.ShapeDtypeStruct((width, depth), BF),
        ),
        in_specs=[vmem] * 4 + [hbm] * 2,
        out_specs=(vmem, vmem, hbm, hbm),
        scratch_shapes=[
            pltpu.VMEM((depth, width), BF),
            pltpu.VMEM((width, depth), BF),
            pltpu.VMEM((NY, 2 * cap, 2 * feat), BF),
            pltpu.VMEM((NY, 2 * cap, 2 * feat), BF),
            pltpu.VMEM((2, 2, half, 2 * feat), BF),
            pltpu.VMEM((NZ, NP, 2, half, 2 * feat), BF),
            pltpu.VMEM((NZ, chunk, width), BF),
            pltpu.VMEM((NZ, chunk, width), BF),
            pltpu.VMEM((NZ, NX, 2, half, 2 * feat), BF),
            pltpu.VMEM((NZ, NX, 2, half, 2 * feat), BF),
            pltpu.VMEM((NZ, NX, 2, half, 2 * feat), BF),
            pltpu.VMEM((NZ, 6, half, 2 * feat), BF),
            pltpu.VMEM((4, 2, half, 2 * feat), BF),
            pltpu.VMEM((NX, 2, half, 2 * feat), BF),
            pltpu.VMEM((NZ // 2, 2, half, 2 * feat), BF),
            pltpu.VMEM((NY, 2 * cap, 2 * feat), BF),
            pltpu.VMEM((NY, 2 * cap, 2 * feat), BF),
            pltpu.VMEM((NP, feat, width), BF),
            pltpu.VMEM((NP, width, feat), BF),
            dma((2,)),
            dma((2, NP)),
            dma((2, NY)),
            dma((2, 4)),
            dma((2, 4)),
            dma((2, 4)),
            dma((2, 4, NZ)),
            dma((2, 4, NZ)),
            dma((2, NZ)),
            dma((2, 6, NZ)),
            dma((2, 4)),
            dma((2, NX)),
            dma((2, 4)),
            dma((2, NY)),
        ],
        compiler_params=pltpu.CompilerParams(
            collective_id=0, has_side_effects=True, vmem_limit_bytes=60 * 1024 * 1024
        ),
        cost_estimate=pl.CostEstimate(
            flops=12 * NZ * chunk * depth * width, bytes_accessed=16 * depth * width, transcendentals=0
        ),
    )(tokens, cotangent, language.reshape(1, rows), owner.reshape(1, langs), w_in, w_out)
    return pl.pallas_call(
        hand_over,
        out_shape=tuple(jax.ShapeDtypeStruct(r.shape, r.dtype) for r in results),
        in_specs=[hbm] * 4,
        out_specs=(hbm,) * 4,
        scratch_shapes=[pltpu.VMEM(r.shape, r.dtype) for r in results] + [dma((2, 4, 4))],
        compiler_params=pltpu.CompilerParams(vmem_limit_bytes=60 * 1024 * 1024),
    )(*results)


def solution(mesh):
    placed = (
        P("dp", "mp"),
        P("dp", "mp"),
        P("dp", None),
        P(),
        P(None, ("dp", "mp")),
        P(("dp", "mp"), None),
    )
    return jax.shard_map(
        shards,
        mesh=mesh,
        in_specs=placed,
        out_specs=(P("dp", "mp"), P("dp", "mp"), P(None, ("dp", "mp")), P(("dp", "mp"), None)),
        check_vma=False,
    )
```

```python
import jax
import jax.numpy as jnp
from jax import lax
from jax.experimental import pallas as pl
from jax.experimental.pallas import tpu as pltpu
from jax.sharding import PartitionSpec as P

MESH = pl.DeviceIdType.MESH
ROOT_HALF = 0.7071067811865476
INV_ROOT_TAU = 0.3989422804014327

NY, NZ, NX, NC = 4, 8, 4, 2
NP = NX * NC
BF = jnp.bfloat16
F32 = jnp.float32


def gelu_pair(hidden):
    normal_cdf = 0.5 * (1.0 + lax.erf(hidden * ROOT_HALF))
    return (
        hidden * normal_cdf,
        normal_cdf + hidden * jnp.exp(-0.5 * hidden * hidden) * INV_ROOT_TAU,
    )


def back_order(e):
    order = (4, 7, 2, 6, 3, 5, 1, 0)
    return sum(i * ((e - k + 8) // 8) * ((k - e + 8) // 8) for k, i in enumerate(order))


def nt_dot(a, b):
    return lax.dot_general(a, b, (((1,), (1,)), ((), ())), preferred_element_type=F32)


def kernel(
    tok, cot, lang, owner, w_in, w_out,
    ffn, gtok, grad_in, grad_out,
    w1, w2, pack, yrecv, zsend, gath, act, hgrad, part, srecv, acc, xrecv, frecv, qrecv, zrecv,
    ysend, yback, gi, go,
    w_sem, g_sem, y_sem, z_sem, f_sem, q_sem, x_sem, s_sem, ps_sem, px_sem, fr_sem, qr_sem, pz_sem,
    py_sem,
):
    dp, mp = lax.axis_index("dp"), lax.axis_index("mp")
    y, z = dp // NZ, dp % NZ
    x, c = mp // NC, mp % NC
    rows, feat = tok.shape
    cell_rows = pack.shape[1]
    cap = cell_rows // 2
    chunk = NY * cap
    half = chunk // 2
    xr, xl, xo = (x + 1) % NX, (x + NX - 1) % NX, (x + 2) % NX
    sib = {"dp": dp, "mp": x * NC + 1 - c}
    right = {"dp": dp, "mp": xr * NC + c}
    left = {"dp": dp, "mp": xl * NC + c}
    ez = 1 - 2 * (z % 2)

    def at_y(k):
        return {"dp": ((y + k) % NY) * NZ + z, "mp": mp}

    def at_z(k):
        return {"dp": y * NZ + (z + k + NZ) % NZ, "mp": mp}

    def remote(src, dst, sems, where, device):
        return pltpu.make_async_remote_copy(
            src_ref=src,
            dst_ref=dst,
            send_sem=sems.at[(0, *where)],
            recv_sem=sems.at[(1, *where)],
            device_id=device,
            device_id_type=MESH,
        )

    load1 = pltpu.make_async_copy(w_in, w1, w_sem.at[0])
    load2 = pltpu.make_async_copy(w_out, w2, w_sem.at[1])
    load1.start()
    load2.start()

    barrier = pltpu.get_barrier_semaphore()
    partners = [sib, right, left] + [at_y(k) for k in range(1, NY)]
    partners += [at_z(k * ez) for k in (1, -1, 2, -2, -3)]
    for device in partners:
        pl.semaphore_signal(barrier, inc=1, device_id=device, device_id_type=MESH)

    langs = owner.shape[1]
    hit = lang[...] == lax.broadcasted_iota(jnp.int32, (langs, rows), 0)
    upper = (
        lax.broadcasted_iota(jnp.int32, (rows, rows), 0)
        < lax.broadcasted_iota(jnp.int32, (rows, rows), 1)
    )
    before = jnp.dot(
        jnp.where(hit, 1.0, 0.0).astype(BF),
        jnp.where(upper, 1.0, 0.0).astype(BF),
        preferred_element_type=F32,
    )
    diagonal = lax.broadcasted_iota(jnp.int32, (langs, langs), 0) == lax.broadcasted_iota(
        jnp.int32, (langs, langs), 1
    )
    slots = jnp.sum(jnp.where(diagonal, owner[...].astype(F32), 0.0), axis=1, keepdims=True)
    cell = jnp.sum(jnp.where(hit, before + slots * cap, 0.0), axis=0, keepdims=True)
    cells = langs * cap
    place_t = jnp.where(
        cell.astype(jnp.int32) == lax.broadcasted_iota(jnp.int32, (cells, rows), 0), 1.0, 0.0
    )
    place = jnp.transpose(place_t).astype(BF)
    place_t = place_t.astype(BF)
    packed_x = jnp.dot(place_t, tok[...], preferred_element_type=F32).astype(BF)
    packed_g = jnp.dot(place_t, cot[...], preferred_element_type=F32).astype(BF)
    pack[:, :, :feat] = packed_x.reshape(NY, cell_rows, feat)
    pack[:, :, feat:] = packed_g.reshape(NY, cell_rows, feat)

    pl.semaphore_wait(barrier, len(partners))

    def y_copy(k):
        return remote(pack.at[(y + k) % NY], yrecv.at[k], y_sem, (k,), at_y(k))

    for k in range(1, NY):
        y_copy(k).start()
    yrecv[0] = pack[y]
    for k in range(1, NY):
        y_copy(k).wait_recv()
    for h in range(2):
        for col in (0, feat):
            block = jnp.concatenate(
                [
                    yrecv[k, :, col : col + feat].astype(F32)[h * cap : (h + 1) * cap]
                    for k in range(NY)
                ],
                axis=0,
            ).astype(BF)
            zsend[h, :, :, col : col + feat] = block.reshape(2, half, feat)

    half_z = NZ // 2
    pair = at_z(ez)

    def z_copy(k):
        to = (z + (0, -ez, 2 * ez, -3 * ez)[k] + NZ) % NZ
        device = {"dp": y * NZ + to, "mp": mp}
        return remote(zsend.at[to // half_z], gath.at[2 * k - 1, mp], z_sem, (k,), device)

    def z_arrived(k):
        return remote(zsend.at[0], gath.at[2 * k - 1, mp], z_sem, (k,), pair)

    def f_copy(k):
        return remote(gath.at[2 * k - 1, mp], gath.at[2 * k, mp], f_sem, (k,), pair)

    def q_copy(kind):
        p = (x, xl, xr, xo)[kind] * NC + c
        return remote(gath.at[0, p], gath.at[NZ - 1, p], q_sem, (kind,), pair)

    z_copy(1).start()
    gath[0, mp] = zsend[z // half_z]

    def g_copy(kind, i):
        if kind == 0:
            return remote(gath.at[i, mp], gath.at[i, mp], x_sem, (0, i), right)
        if kind == 1:
            return remote(gath.at[i, mp], gath.at[i, mp], x_sem, (1, i), left)
        if kind == 2:
            src = gath.at[i, xl * NC + c, 0]
            return remote(src, src, x_sem, (2, i), right)
        src = gath.at[i, xr * NC + c, 1]
        return remote(src, src, x_sem, (3, i), left)

    def s_copy(kind, i):
        src = gath.at[i, (x, xl, xr, xo)[kind] * NC + c]
        return remote(src, src, s_sem, (kind, i), sib)

    def ps_copy(i):
        return remote(part.at[i], srecv.at[i], ps_sem, (i,), sib)

    def p_copy(kind, i):
        where, h, device = (
            (xo, 0, right), (xo, 1, left), (xr, 1, right), (xl, 0, left), (xr, 0, right), (xl, 1, left),
        )[kind]
        return remote(acc.at[i, where, h], xrecv.at[i, kind], px_sem, (kind, i), device)

    def fr_copy(k):
        return remote(acc.at[2 * k, x], frecv.at[k], fr_sem, (k,), pair)

    def qr_copy(q):
        return remote(acc.at[NZ - 1, q], qrecv.at[q], qr_sem, (q,), pair)

    def pz_copy(k):
        return remote(acc.at[2 * k - 1, x], zrecv.at[z // 2], pz_sem, (k,), at_z(-k * ez))

    def pieces(i, p, col):
        return gath[i, p, :, :, col : col + feat].reshape(chunk, feat)

    def w_cols(p):
        return w2[:, pl.ds(pl.multiple_of(p * feat, feat), feat)]

    def w_rows(p):
        return w1[pl.ds(pl.multiple_of(p * feat, feat), feat), :]

    def compute(i):
        width = w1.shape[1]
        hidden = jnp.zeros((chunk, width), F32)
        for p in range(NP):
            hidden += jnp.dot(
                pieces(i, p, 0), w1[p * feat : (p + 1) * feat, :], preferred_element_type=F32
            )
        value, slope = gelu_pair(hidden)
        act[i] = value.astype(BF)
        back = jnp.zeros((chunk, width), F32)
        for p in range(NP):
            back += nt_dot(pieces(i, p, feat), w2[:, p * feat : (p + 1) * feat])
        hgrad[i] = (back * slope).astype(BF)

    def sib_part(i):
        for q in range(NX):
            p = q * NC + 1 - c
            out = jnp.dot(act[i], w_cols(p), preferred_element_type=F32)
            part[i, q, :, :, :feat] = out.astype(BF).reshape(2, half, feat)
            out = nt_dot(hgrad[i], w_rows(p))
            part[i, q, :, :, feat:] = out.astype(BF).reshape(2, half, feat)

    def own_part(i):
        for q in range(NX):
            p = q * NC + c
            out = jnp.dot(act[i], w_cols(p), preferred_element_type=F32).reshape(2, half, feat)
            out += srecv[i, q, :, :, :feat].astype(F32)
            acc[i, q, :, :, :feat] = out.astype(BF)
            out = nt_dot(hgrad[i], w_rows(p)).reshape(2, half, feat)
            out += srecv[i, q, :, :, feat:].astype(F32)
            acc[i, q, :, :, feat:] = out.astype(BF)

    def add_pair(i, q, ref):
        for h in range(2):
            for col in (0, feat):
                total = acc[i, q, h, :, col : col + feat].astype(F32)
                total += ref[h, :, col : col + feat].astype(F32)
                acc[i, q, h, :, col : col + feat] = total.astype(BF)

    def add_to(i, where, h, kinds):
        for col in (0, feat):
            total = acc[i, where, h, :, col : col + feat].astype(F32)
            for kind in kinds:
                total += xrecv[i, kind, :, col : col + feat].astype(F32)
            acc[i, where, h, :, col : col + feat] = total.astype(BF)

    def grads(p):
        hg_t = jnp.transpose(hgrad[...].reshape(NZ * chunk, -1).astype(F32)).astype(BF)
        act_t = jnp.transpose(act[...].reshape(NZ * chunk, -1).astype(F32)).astype(BF)
        xs = gath[:, p, :, :, :feat].reshape(NZ * chunk, feat)
        gs = gath[:, p, :, :, feat:].reshape(NZ * chunk, feat)
        first = jnp.dot(hg_t, xs, preferred_element_type=F32)
        gi[p] = jnp.transpose(first).astype(BF)
        go[p] = jnp.dot(act_t, gs, preferred_element_type=F32).astype(BF)

    def gi_copy(p):
        start = pl.multiple_of(p * feat, feat)
        return pltpu.make_async_copy(gi.at[p], grad_in.at[pl.ds(start, feat), :], g_sem.at[0, p])

    def go_copy(p):
        start = pl.multiple_of(p * feat, feat)
        return pltpu.make_async_copy(go.at[p], grad_out.at[:, pl.ds(start, feat)], g_sem.at[1, p])

    load1.wait()
    load2.wait()

    def stage(t, after, count=NZ):
        return (t >= after) & (t < count + after)

    last = NZ - 1
    first_back = NZ - 1

    @pl.loop(0, NZ + first_back + 3)
    def _(t):
        @pl.when(stage(t, first_back + 1))
        def _():
            i = back_order(t - first_back - 1)
            ps_copy(i).wait_recv()
            own_part(i)

            @pl.when(i == 0)
            def _():
                for q in range(NX):
                    qr_copy(q).wait_recv()
                    add_pair(0, q, qrecv.at[q])

            @pl.when(i < last)
            def _():
                for kind in range(4):
                    p_copy(kind, i).start()

        @pl.when((t >= 2) & (t < last) & (t % 2 == 0))
        def _():
            f_copy(t // 2).wait_recv()

        @pl.when((t < last) & (t % 2 == 1))
        def _():
            k = (t + 1) // 2
            z_arrived(k).wait_recv()
            f_copy(k).start()

        for k in (2, 3):

            @pl.when(t == k)
            def _():
                z_copy(k).start()

        @pl.when(stage(t, 0, last))
        def _():
            g_copy(0, t).start()
            g_copy(1, t).start()
            s_copy(0, t).start()

        @pl.when(stage(t, 1, last))
        def _():
            i = t - 1
            g_copy(0, i).wait_recv()
            g_copy(2, i).start()
            s_copy(1, i).start()
            g_copy(1, i).wait_recv()
            g_copy(3, i).start()
            s_copy(2, i).start()

        @pl.when(stage(t, 2, last))
        def _():
            i = t - 2
            g_copy(2, i).wait_recv()
            g_copy(3, i).wait_recv()
            s_copy(3, i).start()

        for kind in range(4):

            @pl.when(t == min(3 + kind, 5))
            def _():
                q_copy(kind).start()

        @pl.when(t == last)
        def _():
            for kind in range(4):
                q_copy(kind).wait_recv()
                s_copy(kind, last).start()

        @pl.when(stage(t, first_back + 4))
        def _():
            i = back_order(t - first_back - 4)

            @pl.when((i < last) & (i % 2 == 1))
            def _():
                k = (i + 1) // 2
                fr_copy(k).wait_recv()
                add_pair(i, x, frecv.at[k])
                pz_copy(k).start()

        @pl.when(stage(t, first_back + 2))
        def _():
            i = back_order(t - first_back - 2)

            @pl.when(i < last)
            def _():
                p_copy(0, i).wait_recv()
                add_to(i, xr, 0, (0,))
                p_copy(4, i).start()
                p_copy(1, i).wait_recv()
                add_to(i, xl, 1, (1,))
                p_copy(5, i).start()

        for q in range(NX):

            @pl.when(t == last + 2 + q)
            def _():
                qr_copy(q).start()

        @pl.when(stage(t, 3, last))
        def _():
            i = t - 3
            for kind in range(4):
                s_copy(kind, i).wait_recv()
            compute(i)

        @pl.when(t == last + 1)
        def _():
            for kind in range(4):
                s_copy(kind, last).wait_recv()
            compute(last)

        @pl.when(stage(t, first_back))
        def _():
            i = back_order(t - first_back)
            sib_part(i)
            ps_copy(i).start()

        @pl.when(stage(t, first_back + 3))
        def _():
            i = back_order(t - first_back - 3)

            @pl.when(i < last)
            def _():
                for kind in range(2, 6):
                    p_copy(kind, i).wait_recv()
                add_to(i, x, 0, (3, 4))
                add_to(i, x, 1, (2, 5))

            @pl.when((i > 0) & (i % 2 == 0))
            def _():
                fr_copy(i // 2).start()

            @pl.when(i == 0)
            def _():
                zrecv[z // 2] = acc[0, x]

        @pl.when(stage(t, NZ + 2))
        def _():
            p = t - NZ - 2
            grads(p)
            gi_copy(p).start()
            go_copy(p).start()

    for k in (1, 2, 3):
        pz_copy(k).wait_recv()

    for col in (0, feat):
        sums = []
        for h in range(2):
            total = zrecv[2 * h, :, :, col : col + feat].astype(F32)
            total += zrecv[2 * h + 1, :, :, col : col + feat].astype(F32)
            sums.append(total.reshape(chunk, feat))
        for k in range(NY):
            block = jnp.concatenate([s[k * cap : (k + 1) * cap] for s in sums], axis=0)
            ysend[k, :, col : col + feat] = block.astype(BF)

    def yb_copy(k):
        return remote(ysend.at[k], yback.at[y], py_sem, (k,), at_y(NY - k))

    for k in range(1, NY):
        yb_copy(k).start()
    yback[y] = ysend[0]
    for k in range(1, NY):
        yb_copy(k).wait_recv()
    home = yback[...].reshape(cells, 2 * feat)
    ffn[...] = jnp.dot(place, home[:, :feat], preferred_element_type=F32).astype(BF)
    gtok[...] = jnp.dot(place, home[:, feat:], preferred_element_type=F32).astype(BF)

    for k in range(1, NY):
        y_copy(k).wait_send()
        yb_copy(k).wait_send()

        z_copy(k).wait_send()
        f_copy(k).wait_send()
        fr_copy(k).wait_send()
        pz_copy(k).wait_send()
    for kind in range(4):
        q_copy(kind).wait_send()
    for q in range(NX):
        qr_copy(q).wait_send()

    @pl.loop(0, NZ)
    def _(i):
        for kind in range(4):
            s_copy(kind, i).wait_send()
        ps_copy(i).wait_send()

    @pl.loop(0, last)
    def _(i):
        for kind in range(4):
            g_copy(kind, i).wait_send()
        for kind in range(6):
            p_copy(kind, i).wait_send()

    @pl.loop(0, NP)
    def _(p):
        gi_copy(p).wait()
        go_copy(p).wait()


def hand_over(a0, a1, a2, a3, b0, b1, b2, b3, v0, v1, v2, v3, sems):
    moves = []
    for k, (src, mid, dst) in enumerate(((a2, v2, b2), (a3, v3, b3), (a0, v0, b0), (a1, v1, b1))):
        parts = 4 if k < 2 else 1
        size = src.shape[0] // parts
        for n in range(parts):
            rows = pl.ds(n * size, size)
            moves.append(
                (
                    pltpu.make_async_copy(src.at[rows], mid.at[rows], sems.at[0, k, n]),
                    pltpu.make_async_copy(mid.at[rows], dst.at[rows], sems.at[1, k, n]),
                )
            )
    for first, _ in moves:
        first.start()
    for first, second in moves:
        first.wait()
        second.start()
    for _, second in moves:
        second.wait()


def shards(tokens, cotangent, language, owner, w_in, w_out):
    rows, feat = tokens.shape
    depth, width = w_in.shape
    langs = owner.shape[0]
    cap = 3 * rows // (2 * langs)
    chunk = NY * cap
    half = chunk // 2
    vmem, hbm = pl.BlockSpec(memory_space=pltpu.VMEM), pl.BlockSpec(memory_space=pl.ANY)
    dma = pltpu.SemaphoreType.DMA
    results = pl.pallas_call(
        kernel,
        out_shape=(
            jax.ShapeDtypeStruct((rows, feat), BF),
            jax.ShapeDtypeStruct((rows, feat), BF),
            jax.ShapeDtypeStruct((depth, width), BF),
            jax.ShapeDtypeStruct((width, depth), BF),
        ),
        in_specs=[vmem] * 4 + [hbm] * 2,
        out_specs=(vmem, vmem, hbm, hbm),
        scratch_shapes=[
            pltpu.VMEM((depth, width), BF),
            pltpu.VMEM((width, depth), BF),
            pltpu.VMEM((NY, 2 * cap, 2 * feat), BF),
            pltpu.VMEM((NY, 2 * cap, 2 * feat), BF),
            pltpu.VMEM((2, 2, half, 2 * feat), BF),
            pltpu.VMEM((NZ, NP, 2, half, 2 * feat), BF),
            pltpu.VMEM((NZ, chunk, width), BF),
            pltpu.VMEM((NZ, chunk, width), BF),
            pltpu.VMEM((NZ, NX, 2, half, 2 * feat), BF),
            pltpu.VMEM((NZ, NX, 2, half, 2 * feat), BF),
            pltpu.VMEM((NZ, NX, 2, half, 2 * feat), BF),
            pltpu.VMEM((NZ, 6, half, 2 * feat), BF),
            pltpu.VMEM((4, 2, half, 2 * feat), BF),
            pltpu.VMEM((NX, 2, half, 2 * feat), BF),
            pltpu.VMEM((NZ // 2, 2, half, 2 * feat), BF),
            pltpu.VMEM((NY, 2 * cap, 2 * feat), BF),
            pltpu.VMEM((NY, 2 * cap, 2 * feat), BF),
            pltpu.VMEM((NP, feat, width), BF),
            pltpu.VMEM((NP, width, feat), BF),
            dma((2,)),
            dma((2, NP)),
            dma((2, NY)),
            dma((2, 4)),
            dma((2, 4)),
            dma((2, 4)),
            dma((2, 4, NZ)),
            dma((2, 4, NZ)),
            dma((2, NZ)),
            dma((2, 6, NZ)),
            dma((2, 4)),
            dma((2, NX)),
            dma((2, 4)),
            dma((2, NY)),
        ],
        compiler_params=pltpu.CompilerParams(
            collective_id=0, has_side_effects=True, vmem_limit_bytes=60 * 1024 * 1024
        ),
        cost_estimate=pl.CostEstimate(
            flops=12 * NZ * chunk * depth * width, bytes_accessed=16 * depth * width, transcendentals=0
        ),
    )(tokens, cotangent, language.reshape(1, rows), owner.reshape(1, langs), w_in, w_out)
    return pl.pallas_call(
        hand_over,
        out_shape=tuple(jax.ShapeDtypeStruct(r.shape, r.dtype) for r in results),
        in_specs=[hbm] * 4,
        out_specs=(hbm,) * 4,
        scratch_shapes=[pltpu.VMEM(r.shape, r.dtype) for r in results] + [dma((2, 4, 4))],
        compiler_params=pltpu.CompilerParams(vmem_limit_bytes=60 * 1024 * 1024),
    )(*results)


def solution(mesh):
    placed = (
        P("dp", "mp"),
        P("dp", "mp"),
        P("dp", None),
        P(),
        P(None, ("dp", "mp")),
        P(("dp", "mp"), None),
    )
    return jax.shard_map(
        shards,
        mesh=mesh,
        in_specs=placed,
        out_specs=(P("dp", "mp"), P("dp", "mp"), P(None, ("dp", "mp")), P(("dp", "mp"), None)),
        check_vma=False,
    )
```
